32 devices in a mesh: feat: 4 (over y, x), seq: 8 (over z, core).
Axes of the slice: x: 2, y: 2, z: 4, core: 2. Of those that a mesh axis runs over, the one named last changes fastest.
Arguments:
- tokens: bfloat16 [4096, 8192], P('seq', 'feat'), may hold values from -6 to 6
- block_weights: bfloat16 [28672, 512], P('feat'), may hold values from -0.25 to 0.25
- left_factor: bfloat16 [28672, 256], P('feat'), may hold values from -0.09375 to 0.09375
- right_factor: bfloat16 [8192, 256], P('feat'), may hold values from -0.0625 to 0.0625
- pattern: int32 [224, 4], P('feat'), may hold values from 0 to 63, as said below
- cotangent: bfloat16 [4096, 28672], P('seq', 'feat'), may hold values from -6 to 6
Outputs:
- activated: bfloat16 [4096, 28672], P('seq', 'feat')
- grad_input: bfloat16 [8, 512, 8192], P('seq', 'feat')
- grad_blocks: float32 [28672, 512], P(('feat', 'seq'))
- grad_left: float32 [28672, 256], P(('feat', 'seq'))
- grad_right: float32 [8192, 256], P(('feat', 'seq'))
The draws below stay inside these ranges and needn't reach their ends.
Inputs may be any that keep to these rules, and one draw needn't show every extreme that they name: For block row f, pattern[f, 0] // 8 equals (f * 8) // 224, and pattern[f, j] = pattern[f, 0] XOR ((64) >> j) for 1 <= j < 4.
All inputs are finite; a program needn't handle non-finite values.
Results may differ from the reference program's by a relative error of at most 0.0051.
Values may be sent and summed in bfloat16 or wider, within the bound.
No kernel may reach another device: no remote copies, remote signals or barrier semaphores. Data moves between devices by JAX's collectives and lax.ppermute only.
A program may use at most 256 MiB of HBM per device.

```python
import jax
import jax.numpy as jnp
from jax import lax

D = 8192
FF = 28672
R = 256
BLK = 128
LEVELS = 4
TOK_DEV = 512
TOKENS = 4096
N_SEQ = 8


def draw_pattern(key, part):
    row_count = FF // BLK
    col_count = D // BLK
    group_width = col_count // 8
    row_ids = jnp.arange(row_count, dtype=jnp.int32)
    offsets = jax.random.randint(key, (row_count,), 0, group_width, dtype=jnp.int32)
    first_col = row_ids * 8 // row_count * group_width + offsets
    columns = [first_col] + [jnp.bitwise_xor(first_col, col_count >> level) for level in range(1, LEVELS)]
    return jnp.stack(columns, axis=1).astype(jnp.int32)


def spiked(drawn, own_key, source, target, blocks, factor):
    def block_of(position):
        return (jnp.arange(drawn.shape[position]) // (drawn.shape[position] // blocks)).reshape((-1,) + (1,) * (drawn.ndim - 1 - position))

    near = jax.random.permutation(own_key, blocks)[block_of(target)]
    other_side = (block_of(target) + blocks // 2) % blocks
    return jnp.where((block_of(source) == near) | (block_of(source) == other_side), factor * drawn, drawn)


def block_levels(key, extent, cuts, least, largest):
    level, own = 1.0, jax.random.fold_in(key, 6)
    for dim, parts in cuts:
        steps = jnp.exp(jax.random.uniform(jax.random.fold_in(own, dim), (parts,), jnp.float32, least / len(cuts), largest / len(cuts)))
        level = level * jnp.repeat(steps, extent[dim] // parts).reshape([-1 if axis == dim else 1 for axis in range(len(extent))])
    return level


def bell_draw(key, dims, scale, most, shards=(), held_as=jnp.bfloat16):
    drawn = scale * jax.random.normal(key, dims, jnp.float32)
    if shards:
        drawn = drawn * block_levels(key, dims, shards, -0.22, 0.18)
    return jnp.clip(drawn, -most, most).astype(held_as)


def gaussian_with(stream_key, shape, scale, limit, pieces, heavy, kind=jnp.bfloat16):
    entries = scale * jax.random.normal(stream_key, shape, jnp.float32)
    if pieces:
        entries = entries * block_levels(stream_key, shape, pieces, -0.22, 0.18)
    return jnp.clip(spiked(entries, jax.random.fold_in(stream_key, 3), *heavy), -limit, limit).astype(kind)


def setup_inputs(seed: int = 0) -> dict:
    key_of = jax.random.split(jax.random.key(seed), 7)
    tokens = gaussian_with(key_of[0], (TOKENS, D), 1.0, 6.0, ((0, 8), (1, 4)), (0, 1, 8, 2.0))
    block_weights = bell_draw(key_of[1], (FF, LEVELS * BLK), (LEVELS * BLK) ** -0.5, 0.25, ((0, 4),))
    left_factor = bell_draw(key_of[2], (FF, R), (16 * R) ** -0.5, 0.09375, ((0, 4),))
    right_factor = bell_draw(key_of[3], (D, R), D ** -0.5, 0.0625, ((0, 4),))
    pattern = draw_pattern(jax.random.fold_in(key_of[6], 71), 0)
    cotangent = gaussian_with(key_of[5], (TOKENS, FF), 1.0, 6.0, ((0, 8), (1, 4)), (0, 1, 8, 2.0))
    return dict(tokens=tokens, block_weights=block_weights, left_factor=left_factor, right_factor=right_factor, pattern=pattern, cotangent=cotangent)


def activation(values):
    return jax.nn.gelu(values, approximate=True)

def reference(tokens, block_weights, left_factor, right_factor, pattern, cotangent):
    row_blocks = FF // BLK
    col_blocks = D // BLK
    weight_blocks = block_weights.astype(jnp.float32).reshape(row_blocks, BLK, LEVELS, BLK)
    left_wide = left_factor.astype(jnp.float32)
    right_wide = right_factor.astype(jnp.float32)
    tok_blocks = tokens.reshape(N_SEQ, TOK_DEV, D)
    cot_blocks = cotangent.reshape(N_SEQ, TOK_DEV, FF)

    def one_block(carry, inputs):
        sum_blocks, sum_left, sum_right = carry
        tok_block, cot_block = inputs
        picked = tok_block.reshape(TOK_DEV, col_blocks, BLK)[:, pattern, :].astype(jnp.float32)
        sparse = jnp.einsum('tfli,foli->tfo', picked, weight_blocks).reshape(TOK_DEV, FF)
        latent = jnp.dot(tok_block, right_factor, preferred_element_type=jnp.float32).astype(jnp.bfloat16)
        latent_wide = latent.astype(jnp.float32)
        pre = sparse + jnp.einsum('tr,or->to', latent_wide, left_wide)
        activated, slope = jax.vjp(activation, pre)
        grad_pre = slope(cot_block.astype(jnp.float32))[0].astype(jnp.bfloat16)
        grad_wide = grad_pre.astype(jnp.float32)
        back_latent = jnp.einsum('to,or->tr', grad_wide, left_wide).astype(jnp.bfloat16)
        back_wide = back_latent.astype(jnp.float32)
        spread = jnp.einsum('tfo,foli->tfli', grad_wide.reshape(TOK_DEV, row_blocks, BLK), weight_blocks)
        input_sparse = jnp.zeros((TOK_DEV, col_blocks, BLK), jnp.float32).at[:, pattern, :].add(spread)
        input_sum = input_sparse.reshape(TOK_DEV, D) + jnp.einsum('tr,ir->ti', back_wide, right_wide)
        block_term = jnp.einsum('tfo,tfli->foli', grad_wide.reshape(TOK_DEV, row_blocks, BLK), picked)
        sum_blocks = sum_blocks + block_term.reshape(FF, LEVELS * BLK)
        sum_left = sum_left + jnp.einsum('to,tr->or', grad_wide, latent_wide)
        sum_right = sum_right + jnp.einsum('ti,tr->ir', tok_block.astype(jnp.float32), back_wide)
        return ((sum_blocks, sum_left, sum_right), (activated.astype(jnp.bfloat16), input_sum.astype(jnp.bfloat16)))
    start_carry = (jnp.zeros((FF, LEVELS * BLK), jnp.float32), jnp.zeros((FF, R), jnp.float32), jnp.zeros((D, R), jnp.float32))
    sums, outputs = lax.scan(one_block, start_carry, (tok_blocks, cot_blocks))
    norm_scale = TOKENS ** (-0.5)
    activated = outputs[0].reshape(TOKENS, FF)
    grad_input = outputs[1]
    return (activated, grad_input, sums[0] * norm_scale, sums[1] * norm_scale, sums[2] * norm_scale)
```

```python
import functools
import math

import jax
import jax.numpy as jnp
from jax import lax
from jax.experimental import pallas as pl
from jax.experimental.pallas import tpu as pltpu
from jax.sharding import PartitionSpec as P

BLK = 128
LEVELS = 4
GROUPS = 8
STEP = 7
CHUNKS = 4
COST = 30 * 10**9
VMEM = 56 * 1024 * 1024
F32 = jnp.float32
BF16 = jnp.bfloat16
GELU_K = math.sqrt(2.0 / math.pi)
GELU_A = 0.044715


def from_partner(value, axis, distance):
    pairs = [(source, source ^ distance) for source in range(lax.axis_size(axis))]
    return lax.ppermute(value, axis, pairs)


def others(part, axis):
    return [from_partner(part, axis, distance) for distance in range(1, lax.axis_size(axis))]


def forward_kernel(turn, width, pattern_ref, place_ref, *refs):
    slabs = refs[:LEVELS]
    latent_ref, weight_ref, left_ref, cot_ref = refs[LEVELS : LEVELS + 4]
    act_ref, grad_ref, sums_ref, back_ref = refs[-4:]
    step = pl.program_id(0)
    first = chunk_step(place_ref, turn, step) * STEP

    def operands(row):
        column = lax.rem(pattern_ref[first + row, 0], width)
        lanes = pl.ds(pl.multiple_of(column * BLK, BLK), BLK)
        return jnp.concatenate([slab[:, lanes] for slab in slabs] + [latent_ref[...]], axis=1)

    every = [slice(row * BLK, (row + 1) * BLK) for row in range(STEP)]
    pres = []
    for row, rows in enumerate(every):
        weights = jnp.concatenate([weight_ref[rows, :], left_ref[rows, :]], axis=1)
        pres.append(
            lax.dot_general(operands(row), weights, (((1,), (1,)), ((), ())), preferred_element_type=F32)
        )
    grads = []
    for pre, rows in zip(pres, every):
        square = pre * pre
        half = 0.5 + 0.5 * jnp.tanh(pre * (GELU_K + (GELU_K * GELU_A) * square))
        act = pre * half
        act_ref[:, rows] = act.astype(BF16)
        slope = half + act * (1.0 - half) * (2.0 * GELU_K + (6.0 * GELU_K * GELU_A) * square)
        grad = (cot_ref[:, rows].astype(F32) * slope).astype(BF16)
        grad_ref[:, rows] = grad
        grads.append(grad)
    for row, rows in enumerate(every):
        sums_ref[rows, :] = lax.dot_general(
            grads[row], operands(row), (((0,), (0,)), ((), ())), preferred_element_type=F32
        ).astype(BF16)
    back = jnp.dot(jnp.concatenate(grads, axis=1), left_ref[...], preferred_element_type=F32)

    @pl.when(step == 0)
    def _():
        back_ref[...] = back

    @pl.when(step > 0)
    def _():
        back_ref[...] += back


def chunk_step(place, turn, step):
    per_chunk = place[0]
    return place[1 + turn + step // per_chunk] * per_chunk + lax.rem(step, per_chunk)


def chunk_group(place, turn):
    return place[1 + CHUNKS + turn]


def forward_chunk(turn, steps, width, pattern, place, slabs, moves, latent, weights, left, cot, carried, after=()):
    tok_rows, hidden = cot.shape
    rank = left.shape[1]
    wide = STEP * BLK
    rows = steps * wide
    at_slab = lambda move: (lambda i, p, w: (0, 0 if move is None else chunk_group(w, turn) ^ move))
    in_specs = [pl.BlockSpec((tok_rows, width * BLK), at_slab(move)) for move in moves] + [
        pl.BlockSpec((tok_rows, rank), lambda i, p, w: (0, 0)),
        pl.BlockSpec((wide, LEVELS * BLK), lambda i, p, w: (chunk_step(w, turn, i), 0)),
        pl.BlockSpec((wide, rank), lambda i, p, w: (chunk_step(w, turn, i), 0)),
        pl.BlockSpec((tok_rows, wide), lambda i, p, w: (0, chunk_step(w, turn, i))),
    ]
    operands = [pattern, place, *slabs, latent, weights, left, cot]
    aliases = {}
    if carried is not None:
        aliases = {len(operands): 0, len(operands) + 1: 1}
        operands += list(carried)
    operands += list(after)
    in_specs += [pl.BlockSpec(memory_space=pl.ANY)] * (len(operands) - 2 - len(in_specs))
    out_cols = LEVELS * BLK + rank
    return pl.pallas_call(
        functools.partial(forward_kernel, turn, width),
        grid_spec=pltpu.PrefetchScalarGridSpec(
            num_scalar_prefetch=2,
            grid=(steps,),
            in_specs=in_specs,
            out_specs=[
                pl.BlockSpec((tok_rows, wide), lambda i, p, w: (0, chunk_step(w, turn, i))),
                pl.BlockSpec((tok_rows, wide), lambda i, p, w: (0, chunk_step(w, turn, i))),
                pl.BlockSpec((wide, out_cols), lambda i, p, w: (i, 0)),
                pl.BlockSpec((tok_rows, rank), lambda i, p, w: (0, 0)),
            ],
        ),
        out_shape=[
            jax.ShapeDtypeStruct((tok_rows, hidden), BF16),
            jax.ShapeDtypeStruct((tok_rows, hidden), BF16),
            jax.ShapeDtypeStruct((rows, out_cols), BF16),
            jax.ShapeDtypeStruct((tok_rows, rank), F32),
        ],
        input_output_aliases=aliases,
        compiler_params=pltpu.CompilerParams(vmem_limit_bytes=VMEM),
        cost_estimate=pl.CostEstimate(flops=COST, bytes_accessed=24 << 20, transcendentals=0),
        name="forward_chunk",
    )(*operands)


def spread_kernel(turn, steps, width, moves, levels, last, pattern_ref, place_ref, grad_ref, weight_ref, *refs):
    out_ref, total = refs[-2], refs[-1]
    step = pl.program_id(0)
    first = chunk_step(place_ref, turn, step) * STEP
    span = width * BLK

    @pl.when(step == 0)
    def _():
        total[...] = jnp.zeros_like(total)

    weights = weight_ref[...]
    weights = jnp.concatenate([weights[:, level * BLK : (level + 1) * BLK] for level in levels], axis=1)
    for row in range(STEP):
        cols = slice(row * BLK, (row + 1) * BLK)
        column = lax.rem(pattern_ref[first + row, 0], width)
        terms = jnp.dot(grad_ref[:, cols], weights[cols, :], preferred_element_type=F32)
        for at, level in enumerate(levels):
            if last:
                begin = step_group(place_ref, turn, step) ^ moves[level]
            else:
                begin = at
            lanes = pl.ds(pl.multiple_of(begin * span + column * BLK, BLK), BLK)
            total[:, lanes] += terms[:, at * BLK : (at + 1) * BLK]

    @pl.when(step == steps - 1)
    def _():
        value = total[...]
        if last:
            value = value + lax.dot_general(
                refs[0][...], refs[1][...], (((1,), (1,)), ((), ())), preferred_element_type=F32
            )
        out_ref[...] = value.astype(BF16)


def step_group(place, turn, step):
    return place[1 + CHUNKS + turn + step // place[0]]


def spread(turn, steps, width, pattern, place, grad, weights, moves, levels, extra, out_cols, after=()):
    tok_rows = grad.shape[0]
    wide = STEP * BLK
    return pl.pallas_call(
        functools.partial(spread_kernel, turn, steps, width, tuple(moves), tuple(levels), bool(extra)),
        grid_spec=pltpu.PrefetchScalarGridSpec(
            num_scalar_prefetch=2,
            grid=(steps,),
            in_specs=[
                pl.BlockSpec((tok_rows, wide), lambda i, p, w: (0, chunk_step(w, turn, i))),
                pl.BlockSpec((wide, LEVELS * BLK), lambda i, p, w: (chunk_step(w, turn, i), 0)),
            ]
            + [pl.BlockSpec(value.shape, lambda i, p, w: (0, 0)) for value in extra]
            + [pl.BlockSpec(memory_space=pl.ANY)] * len(after),
            out_specs=pl.BlockSpec((tok_rows, out_cols), lambda i, p, w: (0, 0)),
            scratch_shapes=[pltpu.VMEM((tok_rows, out_cols), F32)],
        ),
        out_shape=jax.ShapeDtypeStruct((tok_rows, out_cols), BF16),
        compiler_params=pltpu.CompilerParams(vmem_limit_bytes=VMEM),
        cost_estimate=pl.CostEstimate(flops=COST, bytes_accessed=24 << 20, transcendentals=0),
        name="spread",
    )(pattern, place, grad, weights, *extra, *after)


def merge_kernel(remote, distances, span, place_ref, own_ref, *refs):
    sources, out_ref = refs[:-1], refs[-1]
    owner = pl.program_id(0)
    for turn in range(len(sources)):
        lanes = pl.ds(pl.multiple_of((chunk_group(place_ref, 0) ^ turn) * span, span), span)
        total = own_ref[owner, :, lanes].astype(F32)
        for at, level in enumerate(remote):
            total = total + sources[turn][owner ^ distances[level], :, at * span : (at + 1) * span].astype(F32)
        out_ref[0, :, lanes] = total.astype(BF16)


def merge_terms(place, own, arrived, remote, distances, span):
    count, rows, width = own.shape
    return pl.pallas_call(
        functools.partial(merge_kernel, tuple(remote), tuple(distances), span),
        grid_spec=pltpu.PrefetchScalarGridSpec(
            num_scalar_prefetch=1,
            grid=(count,),
            in_specs=[pl.BlockSpec(value.shape, lambda q, w: (0, 0, 0)) for value in (own, *arrived)],
            out_specs=pl.BlockSpec((1, rows, width), lambda q, w: (0, 0, q)),
        ),
        out_shape=jax.ShapeDtypeStruct((1, rows, count * width), BF16),
        compiler_params=pltpu.CompilerParams(vmem_limit_bytes=VMEM),
        name="merge_terms",
    )(place, own, *arrived)


def right_kernel(bits, rows, place_ref, tokens_ref, back_ref, keep_ref, send_ref):
    even = place_ref[1 + 2 * CHUNKS] == 0
    for turn in range(CHUNKS):
        for pair in range(1 << (bits - 1)):
            begin = ((place_ref[1 + turn] << (bits - 1)) + pair) * 2 * rows
            lanes = pl.ds(pl.multiple_of(begin, 2 * rows), 2 * rows)
            both = lax.dot_general(
                tokens_ref[:, lanes], back_ref[...], (((0,), (0,)), ((), ())), preferred_element_type=F32
            )
            low, high = both[:rows], both[rows:]
            at = slice(pair * rows, (pair + 1) * rows)
            keep_ref[turn, at, :] = jnp.where(even, low, high).astype(BF16)
            send_ref[turn, at, :] = jnp.where(even, high, low).astype(BF16)


def right_sums(bits, count, place, tokens, back):
    rows = tokens.shape[1] // count
    shape = jax.ShapeDtypeStruct((CHUNKS, rows << (bits - 1), back.shape[1]), BF16)
    return pl.pallas_call(
        functools.partial(right_kernel, bits, rows),
        grid_spec=pltpu.PrefetchScalarGridSpec(
            num_scalar_prefetch=1,
            grid=(1,),
            in_specs=[pl.BlockSpec(value.shape, lambda i, w: (0, 0)) for value in (tokens, back)],
            out_specs=[pl.BlockSpec(shape.shape, lambda i, w: (0, 0, 0))] * 2,
        ),
        out_shape=[shape, shape],
        compiler_params=pltpu.CompilerParams(vmem_limit_bytes=VMEM),
        name="right_sums",
    )(place, tokens, back)


def pair_sums(value, other, index, bits):
    count = 1 << bits
    rows = value.shape[0] // count
    split = lambda v: v.reshape(count // 2, 2, rows, v.shape[1])
    mine = lambda v: lax.dynamic_index_in_dim(split(v), index & 1, 1, keepdims=False).astype(F32)
    return lower_sums(mine(value) + mine(other), index, bits)


def lower_sums(part, index, bits):
    for bit in range(1, bits):
        mine = (index >> bit) & 1
        part = part.reshape(part.shape[0] // 2, 2, *part.shape[1:])
        keep = lax.dynamic_index_in_dim(part, mine, 1, keepdims=False)
        send = lax.dynamic_index_in_dim(part, 1 - mine, 1, keepdims=False)
        part = keep + from_partner(send.astype(BF16), "seq", 1 << bit).astype(F32)
    return part[0]


def local(tokens, block_weights, left_factor, right_factor, pattern, cotangent):
    tok_rows, local_width = tokens.shape
    feat_count = lax.axis_size("feat")
    seq_count = lax.axis_size("seq")
    norm_scale = 1.0 / math.sqrt(tok_rows * seq_count)
    local_blocks = local_width // BLK
    width = local_blocks * feat_count // GROUPS
    groups = local_blocks // width
    rows = pattern.shape[0] // groups
    span = width * BLK
    strides = [0] + [GROUPS >> level for level in range(1, LEVELS)]
    distances = [stride // groups for stride in strides]
    moves = [stride if stride < groups else 0 for stride in strides]

    index = lax.axis_index("seq")
    bits = seq_count.bit_length() - 3
    near, far = 1 << bits, 2 << bits
    quarter = index >> bits

    latent_part = jnp.dot(tokens, right_factor, preferred_element_type=F32)
    distance = feat_count // 2
    other = from_partner(latent_part.astype(BF16), "feat", distance)
    tokens_after, other = lax.optimization_barrier((tokens, other))
    received = []
    for turn in range(groups):
        group = (quarter ^ (CHUNKS - 1)) * groups // CHUNKS ^ turn
        piece = lax.dynamic_slice_in_dim(tokens, group * span, span, 1)
        late = lax.dynamic_slice_in_dim(tokens_after, group * span, span, 1)
        sources = [late if turn > 0 or d == feat_count // 2 else piece for d in distances]
        received.append([from_partner(s, "feat", d) if d > 0 else None for s, d in zip(sources, distances)])
        if turn == 0:
            latent_part = latent_part + other.astype(F32)
            while distance > 1:
                distance //= 2
                tokens_after, latent_part = lax.optimization_barrier((tokens_after, latent_part))
                latent_part = latent_part + from_partner(latent_part.astype(BF16), "feat", distance).astype(F32)
    latent = latent_part.astype(BF16)

    remote = [level for level in range(LEVELS) if distances[level] > 0]
    slots = [None if d > 0 else move for d, move in zip(distances, moves)]
    steps = pattern.shape[0] // STEP // CHUNKS
    turns = CHUNKS // groups
    part_rows = tok_rows // feat_count

    def to_owner(value):
        value = value.reshape(feat_count, part_rows, value.shape[1])
        return lax.all_to_all(value, "feat", split_axis=0, concat_axis=0, tiled=True)

    chunks = [quarter ^ (CHUNKS - 1 - turn) for turn in range(CHUNKS)]
    place = jnp.stack([jnp.int32(steps)] + chunks + [chunk * groups // CHUNKS for chunk in chunks] + [index & 1]).astype(jnp.int32)

    def forward(turn, count, carried, after=()):
        slabs = [tokens if slab is None else slab for slab in received[turn // turns]]
        return forward_chunk(
            turn, steps * count, width, pattern, place, slabs, slots, latent, block_weights, left_factor, cotangent,
            carried, after,
        )

    def spread_levels(turn, count, grad, levels, extra, out_cols, after=()):
        return spread(
            turn, steps * count, width, pattern, place, grad, block_weights, moves, levels, extra, out_cols, after
        )

    hold = lax.optimization_barrier
    near_hop = lambda value: from_partner(value, "seq", near)
    far_hop = lambda value: from_partner(value, "seq", far)

    def line_hop(value, routes):
        low = range(near)
        pairs = [(a * near + at, b * near + at) for a, b in routes for at in low]
        return lax.ppermute(value, "seq", pairs)

    inward = lambda value: line_hop(value, [(0, 1), (3, 2)])
    across = lambda value: line_hop(value, [(1, 2), (2, 1)])
    core_hop = lambda value: from_partner(value, "seq", 1)
    wide = lambda value: value.astype(F32)

    act, grad, total0, back0 = forward(0, 1, None)
    swap0 = core_hop(total0)
    act, grad, total1, back1 = forward(1, 1, (act, grad), [slab for slab in received[-1] if slab is not None])
    grad, total1, swap0 = hold((grad, total1, swap0))

    sum0 = pair_sums(total0, swap0, index, bits).astype(BF16)
    got0 = inward(sum0)
    swap1 = core_hop(total1)
    arrived = []
    if groups > 1:
        terms = spread_levels(0, turns, grad, remote, (), len(remote) * span)
        terms, swap1, grad = hold((terms, swap1, grad))
        arrived.append(to_owner(terms))
    sum1 = pair_sums(total1, swap1, index, bits).astype(BF16)
    got1 = inward(sum1)
    act, grad, total2, back2 = forward(2, 1, (act, grad))
    grad, total2, back2, got0 = hold((grad, total2, back2, got0))

    got2 = across((wide(sum1) + wide(got0)).astype(BF16))
    swap2 = core_hop(total2)
    act, grad, total3, back3 = forward(3, 1, (act, grad))
    grad, total3, back3, swap2, arrived = hold((grad, total3, back3, swap2, arrived))

    swap3 = core_hop(total3)
    back = back0 + back1 + back2 + back3
    parts = others(back.astype(BF16), "feat")
    sum2 = pair_sums(total2, swap2, index, bits)
    terms = spread_levels(CHUNKS - turns, turns, grad, remote, (), len(remote) * span)
    terms, swap3, parts, got1, got2, grad = hold((terms, swap3, parts, got1, got2, grad))

    for part in parts:
        back = back + wide(part)
    back_latent = back.astype(BF16)
    got3 = across((wide(sum0) + wide(got1)).astype(BF16))
    got4 = near_hop((sum2 + wide(got2)).astype(BF16))
    arrived.append(to_owner(terms))
    right_keep, right_send = right_sums(bits, seq_count, place, tokens, back_latent)
    right_swap = core_hop(right_send)
    own_levels = [level for level in range(LEVELS) if level not in remote]
    own = spread_levels(0, CHUNKS, grad, own_levels, (back_latent, right_factor), local_width)
    own, right_swap = hold((own, right_swap))

    own = to_owner(own)
    right = wide(right_keep) + wide(right_swap)
    right = jnp.stack(
        [lower_sums(part.reshape(1 << (bits - 1), -1, part.shape[1]), index, bits) for part in right]
    )
    close = near_hop(right[0::2].astype(BF16))
    grad_right = right[3] + wide(close[1]) + wide(far_hop((right[1] + wide(close[0])).astype(BF16)))
    grad_right = grad_right * norm_scale
    final = pair_sums(total3, swap3, index, bits) + wide(got3) + wide(got4)
    final = final * norm_scale
    grad_input = merge_terms(place, own, arrived, remote, distances, span)

    return (act, grad_input, final[:, : LEVELS * BLK], final[:, LEVELS * BLK :], grad_right)


def solution(mesh):
    in_specs = (
        P("seq", "feat"),
        P("feat", None),
        P("feat", None),
        P("feat", None),
        P("feat", None),
        P("seq", "feat"),
    )
    out_specs = (
        P("seq", "feat"),
        P("seq", "feat", None),
        P(("feat", "seq"), None),
        P(("feat", "seq"), None),
        P(("feat", "seq"), None),
    )
    return jax.shard_map(local, mesh=mesh, in_specs=in_specs, out_specs=out_specs, check_vma=False)
```

```python
import functools
import math

import jax
import jax.numpy as jnp
from jax import lax
from jax.experimental import pallas as pl
from jax.experimental.pallas import tpu as pltpu
from jax.sharding import PartitionSpec as P

BLK = 128
LEVELS = 4
GROUPS = 8
STEP = 7
CHUNKS = 4
COST = 30 * 10**9
VMEM = 56 * 1024 * 1024
F32 = jnp.float32
BF16 = jnp.bfloat16
GELU_K = math.sqrt(2.0 / math.pi)
GELU_A = 0.044715


def from_partner(value, axis, distance):
    pairs = [(source, source ^ distance) for source in range(lax.axis_size(axis))]
    return lax.ppermute(value, axis, pairs)


def others(part, axis):
    return [from_partner(part, axis, distance) for distance in range(1, lax.axis_size(axis))]


def forward_kernel(turn, width, pattern_ref, place_ref, *refs):
    slabs = refs[:LEVELS]
    latent_ref, weight_ref, left_ref, cot_ref = refs[LEVELS : LEVELS + 4]
    act_ref, grad_ref, sums_ref, back_ref = refs[-4:]
    step = pl.program_id(0)
    first = chunk_step(place_ref, turn, step) * STEP

    def picked(row):
        column = lax.rem(pattern_ref[first + row, 0], width)
        lanes = pl.ds(pl.multiple_of(column * BLK, BLK), BLK)
        return jnp.concatenate([slab[:, lanes] for slab in slabs], axis=1)

    across = (((1,), (1,)), ((), ()))
    along = (((0,), (0,)), ((), ()))
    every = [slice(row * BLK, (row + 1) * BLK) for row in range(STEP)]
    low = lax.dot_general(latent_ref[...], left_ref[...], across, preferred_element_type=F32)
    pres = []
    for row, rows in enumerate(every):
        sparse = lax.dot_general(picked(row), weight_ref[rows, :], across, preferred_element_type=F32)
        pres.append(sparse + low[:, rows])
    grads = []
    for pre, rows in zip(pres, every):
        square = pre * pre
        half = 0.5 + 0.5 * jnp.tanh(pre * (GELU_K + (GELU_K * GELU_A) * square))
        act = pre * half
        act_ref[:, rows] = act.astype(BF16)
        slope = half + act * (1.0 - half) * (2.0 * GELU_K + (6.0 * GELU_K * GELU_A) * square)
        grad = (cot_ref[:, rows].astype(F32) * slope).astype(BF16)
        grad_ref[:, rows] = grad
        grads.append(grad)
    sparse_cols = LEVELS * BLK
    for row, rows in enumerate(every):
        sums_ref[rows, :sparse_cols] = lax.dot_general(
            grads[row], picked(row), along, preferred_element_type=F32
        ).astype(BF16)
    grads = jnp.concatenate(grads, axis=1)
    sums_ref[:, sparse_cols:] = lax.dot_general(
        grads, latent_ref[...], along, preferred_element_type=F32
    ).astype(BF16)
    back = jnp.dot(grads, left_ref[...], preferred_element_type=F32)

    @pl.when(step == 0)
    def _():
        back_ref[...] = back

    @pl.when(step > 0)
    def _():
        back_ref[...] += back


def chunk_step(place, turn, step):
    per_chunk = place[0]
    return place[1 + turn + step // per_chunk] * per_chunk + lax.rem(step, per_chunk)


def chunk_group(place, turn):
    return place[1 + CHUNKS + turn]


def forward_chunk(turn, steps, width, pattern, place, slabs, moves, latent, weights, left, cot, carried, after=()):
    tok_rows, hidden = cot.shape
    rank = left.shape[1]
    wide = STEP * BLK
    rows = steps * wide
    at_slab = lambda move: (lambda i, p, w: (0, 0 if move is None else chunk_group(w, turn) ^ move))
    in_specs = [pl.BlockSpec((tok_rows, width * BLK), at_slab(move)) for move in moves] + [
        pl.BlockSpec((tok_rows, rank), lambda i, p, w: (0, 0)),
        pl.BlockSpec((wide, LEVELS * BLK), lambda i, p, w: (chunk_step(w, turn, i), 0)),
        pl.BlockSpec((wide, rank), lambda i, p, w: (chunk_step(w, turn, i), 0)),
        pl.BlockSpec((tok_rows, wide), lambda i, p, w: (0, chunk_step(w, turn, i))),
    ]
    operands = [pattern, place, *slabs, latent, weights, left, cot]
    aliases = {}
    if carried is not None:
        aliases = {len(operands): 0, len(operands) + 1: 1}
        operands += list(carried)
    operands += list(after)
    in_specs += [pl.BlockSpec(memory_space=pl.ANY)] * (len(operands) - 2 - len(in_specs))
    out_cols = LEVELS * BLK + rank
    return pl.pallas_call(
        functools.partial(forward_kernel, turn, width),
        grid_spec=pltpu.PrefetchScalarGridSpec(
            num_scalar_prefetch=2,
            grid=(steps,),
            in_specs=in_specs,
            out_specs=[
                pl.BlockSpec((tok_rows, wide), lambda i, p, w: (0, chunk_step(w, turn, i))),
                pl.BlockSpec((tok_rows, wide), lambda i, p, w: (0, chunk_step(w, turn, i))),
                pl.BlockSpec((wide, out_cols), lambda i, p, w: (i, 0)),
                pl.BlockSpec((tok_rows, rank), lambda i, p, w: (0, 0)),
            ],
        ),
        out_shape=[
            jax.ShapeDtypeStruct((tok_rows, hidden), BF16),
            jax.ShapeDtypeStruct((tok_rows, hidden), BF16),
            jax.ShapeDtypeStruct((rows, out_cols), BF16),
            jax.ShapeDtypeStruct((tok_rows, rank), F32),
        ],
        input_output_aliases=aliases,
        compiler_params=pltpu.CompilerParams(vmem_limit_bytes=VMEM),
        cost_estimate=pl.CostEstimate(flops=COST, bytes_accessed=24 << 20, transcendentals=0),
        name="forward_chunk",
    )(*operands)


def spread_kernel(turn, steps, width, moves, levels, last, pattern_ref, place_ref, grad_ref, weight_ref, *refs):
    out_ref, total = refs[-2], refs[-1]
    step = pl.program_id(0)
    first = chunk_step(place_ref, turn, step) * STEP
    span = width * BLK

    @pl.when(step == 0)
    def _():
        total[...] = jnp.zeros_like(total)

    weights = weight_ref[...]
    weights = jnp.concatenate([weights[:, level * BLK : (level + 1) * BLK] for level in levels], axis=1)
    every = [slice(row * BLK, (row + 1) * BLK) for row in range(STEP)]
    terms = [jnp.dot(grad_ref[:, cols], weights[cols, :], preferred_element_type=F32) for cols in every]
    for row in range(STEP):
        column = lax.rem(pattern_ref[first + row, 0], width)
        for at, level in enumerate(levels):
            begin = step_group(place_ref, turn, step) ^ moves[level] if last else at
            lanes = pl.ds(pl.multiple_of(begin * span + column * BLK, BLK), BLK)
            total[:, lanes] += terms[row][:, at * BLK : (at + 1) * BLK]

    @pl.when(step == steps - 1)
    def _():
        value = total[...]
        if last:
            value = value + lax.dot_general(
                refs[0][...], refs[1][...], (((1,), (1,)), ((), ())), preferred_element_type=F32
            )
        out_ref[...] = value.astype(BF16)


def step_group(place, turn, step):
    return place[1 + CHUNKS + turn + step // place[0]]


def spread(turn, steps, width, pattern, place, grad, weights, moves, levels, extra, out_cols, after=()):
    tok_rows = grad.shape[0]
    wide = STEP * BLK
    return pl.pallas_call(
        functools.partial(spread_kernel, turn, steps, width, tuple(moves), tuple(levels), bool(extra)),
        grid_spec=pltpu.PrefetchScalarGridSpec(
            num_scalar_prefetch=2,
            grid=(steps,),
            in_specs=[
                pl.BlockSpec((tok_rows, wide), lambda i, p, w: (0, chunk_step(w, turn, i))),
                pl.BlockSpec((wide, LEVELS * BLK), lambda i, p, w: (chunk_step(w, turn, i), 0)),
            ]
            + [pl.BlockSpec(value.shape, lambda i, p, w: (0, 0)) for value in extra]
            + [pl.BlockSpec(memory_space=pl.ANY)] * len(after),
            out_specs=pl.BlockSpec((tok_rows, out_cols), lambda i, p, w: (0, 0)),
            scratch_shapes=[pltpu.VMEM((tok_rows, out_cols), F32)],
        ),
        out_shape=jax.ShapeDtypeStruct((tok_rows, out_cols), BF16),
        compiler_params=pltpu.CompilerParams(vmem_limit_bytes=VMEM),
        cost_estimate=pl.CostEstimate(flops=COST, bytes_accessed=24 << 20, transcendentals=0),
        name="spread",
    )(pattern, place, grad, weights, *extra, *after)


def merge_kernel(remote, distances, span, place_ref, own_ref, *refs):
    sources, out_ref = refs[:-1], refs[-1]
    owner = pl.program_id(0)
    for turn in range(len(sources)):
        lanes = pl.ds(pl.multiple_of((chunk_group(place_ref, 0) ^ turn) * span, span), span)
        total = own_ref[owner, :, lanes].astype(F32)
        for at, level in enumerate(remote):
            total = total + sources[turn][owner ^ distances[level], :, at * span : (at + 1) * span].astype(F32)
        out_ref[0, :, lanes] = total.astype(BF16)


def merge_terms(place, own, arrived, remote, distances, span):
    count, rows, width = own.shape
    return pl.pallas_call(
        functools.partial(merge_kernel, tuple(remote), tuple(distances), span),
        grid_spec=pltpu.PrefetchScalarGridSpec(
            num_scalar_prefetch=1,
            grid=(count,),
            in_specs=[pl.BlockSpec(value.shape, lambda q, w: (0, 0, 0)) for value in (own, *arrived)],
            out_specs=pl.BlockSpec((1, rows, width), lambda q, w: (0, 0, q)),
        ),
        out_shape=jax.ShapeDtypeStruct((1, rows, count * width), BF16),
        compiler_params=pltpu.CompilerParams(vmem_limit_bytes=VMEM),
        name="merge_terms",
    )(place, own, *arrived)


def right_kernel(place_ref, tokens_ref, back_ref, *outs):
    cols = outs[0].shape[1]
    for turn in range(CHUNKS):
        lanes = pl.ds(pl.multiple_of(place_ref[1 + turn] * cols, cols), cols)
        outs[turn % 2][turn // 2] = lax.dot_general(
            tokens_ref[:, lanes], back_ref[...], (((0,), (0,)), ((), ())), preferred_element_type=F32
        ).astype(BF16)


def right_sums(place, tokens, back):
    shape = jax.ShapeDtypeStruct((CHUNKS // 2, tokens.shape[1] // CHUNKS, back.shape[1]), BF16)
    return pl.pallas_call(
        right_kernel,
        grid_spec=pltpu.PrefetchScalarGridSpec(
            num_scalar_prefetch=1,
            grid=(1,),
            in_specs=[pl.BlockSpec(value.shape, lambda i, w: (0, 0)) for value in (tokens, back)],
            out_specs=[pl.BlockSpec(shape.shape, lambda i, w: (0, 0, 0))] * 2,
        ),
        out_shape=[shape, shape],
        compiler_params=pltpu.CompilerParams(vmem_limit_bytes=VMEM),
        name="right_sums",
    )(place, tokens, back)


def pair_kernel(place_ref, *refs):
    for mine, other, out in zip(refs[:2], refs[2:4], refs[4:]):
        out[...] = (mine[...].astype(F32) + other[...].astype(F32)).astype(out.dtype)


def pair_sums(place, total, swapped, index, bits, dtypes):
    count = 1 << bits
    rows = total.shape[0] // 2 // count
    cols = total.shape[1]
    block = (rows // 2, cols)
    specs = [
        pl.BlockSpec(block, lambda i, h, w, turn=turn: ((turn * count + 2 * i + w[1 + 2 * CHUNKS]) * 2 + h, 0))
        for turn in (0, 1)
    ]
    sums = pl.pallas_call(
        pair_kernel,
        grid_spec=pltpu.PrefetchScalarGridSpec(
            num_scalar_prefetch=1,
            grid=(count // 2, 2),
            in_specs=specs * 2,
            out_specs=[pl.BlockSpec(block, lambda i, h, w: (2 * i + h, 0))] * 2,
        ),
        out_shape=[jax.ShapeDtypeStruct((rows * count // 2, cols), dtype) for dtype in dtypes],
        name="pair_sums",
    )(place, total, total, swapped, swapped)
    if bits == 1:
        return sums
    return [lower_sums(part.astype(F32).reshape(count // 2, rows, cols), index, 1, bits).astype(part.dtype) for part in sums]


def final_kernel(scale, kept_ref, first_ref, second_ref, blocks_ref, left_ref):
    total = kept_ref[...] + first_ref[...].astype(F32) + second_ref[...].astype(F32)
    total = total * scale
    cols = blocks_ref.shape[1]
    blocks_ref[...] = total[:, :cols]
    left_ref[...] = total[:, cols:]


def final_sums(kept, first, second, scale):
    rows, cols = kept.shape
    split = LEVELS * BLK
    block = lambda width: pl.BlockSpec((rows // 2, width), lambda h: (h, 0))
    return pl.pallas_call(
        functools.partial(final_kernel, scale),
        grid=(2,),
        in_specs=[block(cols)] * 3,
        out_specs=[block(split), block(cols - split)],
        out_shape=[jax.ShapeDtypeStruct((rows, width), F32) for width in (split, cols - split)],
        name="final_sums",
    )(kept, first, second)


def lower_sums(part, index, first, bits):
    for bit in range(first, bits):
        mine = (index >> bit) & 1
        part = part.reshape(part.shape[0] // 2, 2, *part.shape[1:])
        keep = lax.dynamic_index_in_dim(part, mine, 1, keepdims=False)
        send = lax.dynamic_index_in_dim(part, 1 - mine, 1, keepdims=False)
        part = keep + from_partner(send.astype(BF16), "seq", 1 << bit).astype(F32)
    return part[0]


def local(tokens, block_weights, left_factor, right_factor, pattern, cotangent):
    tok_rows, local_width = tokens.shape
    feat_count = lax.axis_size("feat")
    seq_count = lax.axis_size("seq")
    norm_scale = 1.0 / math.sqrt(tok_rows * seq_count)
    local_blocks = local_width // BLK
    width = local_blocks * feat_count // GROUPS
    groups = local_blocks // width
    rows = pattern.shape[0] // groups
    span = width * BLK
    strides = [0] + [GROUPS >> level for level in range(1, LEVELS)]
    distances = [stride // groups for stride in strides]
    moves = [stride if stride < groups else 0 for stride in strides]

    index = lax.axis_index("seq")
    bits = seq_count.bit_length() - 3
    near, far = 1 << bits, 2 << bits
    quarter = index >> bits

    latent_part = jnp.dot(tokens, right_factor, preferred_element_type=F32)
    distance = feat_count // 2
    other = from_partner(latent_part.astype(BF16), "feat", distance)
    received = []
    for turn in range(groups):
        group = (quarter ^ (CHUNKS - 1)) * groups // CHUNKS ^ turn
        piece = lax.dynamic_slice_in_dim(tokens, group * span, span, 1)
        if turn == 0:
            late, other = lax.optimization_barrier((piece, other))
        else:
            piece, latent_part = lax.optimization_barrier((piece, latent_part))
            late = piece
        sources = [late if d == feat_count // 2 else piece for d in distances]
        received.append([from_partner(s, "feat", d) if d > 0 else None for s, d in zip(sources, distances)])
        if turn == 0:
            latent_part = latent_part + other.astype(F32)
            while distance > 1:
                distance //= 2
                latent_part = latent_part + from_partner(latent_part.astype(BF16), "feat", distance).astype(F32)
    latent = latent_part.astype(BF16)

    remote = [level for level in range(LEVELS) if distances[level] > 0]
    slots = [None if d > 0 else move for d, move in zip(distances, moves)]
    steps = pattern.shape[0] // STEP // CHUNKS
    turns = CHUNKS // groups
    part_rows = tok_rows // feat_count

    def to_owner(value):
        value = value.reshape(feat_count, part_rows, value.shape[1])
        return lax.all_to_all(value, "feat", split_axis=0, concat_axis=0, tiled=True)

    chunks = [quarter ^ (CHUNKS - 1 - turn) for turn in range(CHUNKS)]
    place = jnp.stack([jnp.int32(steps)] + chunks + [chunk * groups // CHUNKS for chunk in chunks] + [index & 1]).astype(jnp.int32)

    def forward(turn, count, carried, after=()):
        slabs = [tokens if slab is None else slab for slab in received[turn // turns]]
        return forward_chunk(
            turn, steps * count, width, pattern, place, slabs, slots, latent, block_weights, left_factor, cotangent,
            carried, after,
        )

    def spread_levels(turn, count, grad, levels, extra, out_cols, after=()):
        return spread(
            turn, steps * count, width, pattern, place, grad, block_weights, moves, levels, extra, out_cols, after
        )

    hold = lax.optimization_barrier
    near_hop = lambda value: from_partner(value, "seq", near)
    far_hop = lambda value: from_partner(value, "seq", far)

    def line_hop(value, routes):
        low = range(near)
        pairs = [(a * near + at, b * near + at) for a, b in routes for at in low]
        return lax.ppermute(value, "seq", pairs)

    inward = lambda value: line_hop(value, [(0, 1), (3, 2)])
    across = lambda value: line_hop(value, [(1, 2), (2, 1)])
    core_hop = lambda value: from_partner(value, "seq", 1)
    wide = lambda value: value.astype(F32)

    act, grad, total, back = forward(0, 2, None)
    if groups > 1:
        received[1], total, grad = hold((received[1], total, grad))
    swapped = core_hop(total)
    arrived = []
    if groups > 1:
        terms = spread_levels(0, turns, grad, remote, (), len(remote) * span)
        terms, swapped, grad = hold((terms, swapped, grad))
    sum0, sum1 = pair_sums(place, total, swapped, index, bits, (BF16, BF16))
    got0, got1 = inward(sum0), inward(sum1)
    if groups > 1:
        arrived.append(to_owner(terms))
    act, grad, total, more = forward(2, 2, (act, grad))
    grad, total, more, got0, arrived = hold((grad, total, more, got0, arrived))

    got2 = across((wide(sum1) + wide(got0)).astype(BF16))
    back = back + more
    parts = others(back.astype(BF16), "feat")
    swapped = core_hop(total)
    terms = spread_levels(CHUNKS - turns, turns, grad, remote, (), len(remote) * span)
    terms, swapped, parts, grad = hold((terms, swapped, parts, grad))

    for part in parts:
        back = back + wide(part)
    back_latent = back.astype(BF16)
    right_send, right_keep = right_sums(place, tokens, back_latent)
    close = near_hop(right_send)
    arrived.append(to_owner(terms))
    sum2, sum3 = pair_sums(place, total, swapped, index, bits, (BF16, F32))
    own_levels = [level for level in range(LEVELS) if level not in remote]
    own = spread_levels(0, CHUNKS, grad, own_levels, (back_latent, right_factor), local_width, (sum3,))
    own, close, got1, got2 = hold((own, close, got1, got2))

    last_part = far_hop((wide(right_keep[0]) + wide(close[0])).astype(BF16))
    own = to_owner(own)
    send4 = (wide(sum2) + wide(got2)).astype(BF16)
    send3 = (wide(sum0) + wide(got1)).astype(BF16)
    send4, send3, last_part = hold((send4, send3, last_part))
    got4 = near_hop(send4)
    got3 = across(send3)
    right = wide(right_keep[1]) + wide(close[1]) + wide(last_part)
    grad_right = lower_sums(right.reshape(1 << bits, -1, right.shape[1]), index, 0, bits) * norm_scale
    grad_input = merge_terms(place, own, arrived, remote, distances, span)
    grad_input, grad_right, got3, got4 = hold((grad_input, grad_right, got3, got4))
    grad_blocks, grad_left = final_sums(sum3, got3, got4, norm_scale)

    return (act, grad_input, grad_blocks, grad_left, grad_right)


def solution(mesh):
    in_specs = (
        P("seq", "feat"),
        P("feat", None),
        P("feat", None),
        P("feat", None),
        P("feat", None),
        P("seq", "feat"),
    )
    out_specs = (
        P("seq", "feat"),
        P("seq", "feat", None),
        P(("feat", "seq"), None),
        P(("feat", "seq"), None),
        P(("feat", "seq"), None),
    )
    return jax.shard_map(local, mesh=mesh, in_specs=in_specs, out_specs=out_specs, check_vma=False)
```

```python
import functools
import math

import jax
import jax.numpy as jnp
from jax import lax
from jax.experimental import pallas as pl
from jax.experimental.pallas import tpu as pltpu
from jax.sharding import PartitionSpec as P

BLK = 128
LEVELS = 4
GROUPS = 8
STEP = 7
CHUNKS = 4
COST = 30 * 10**9
VMEM = 56 * 1024 * 1024
F32 = jnp.float32
BF16 = jnp.bfloat16
GELU_K = math.sqrt(2.0 / math.pi)
GELU_A = 0.044715


def from_partner(value, axis, distance):
    pairs = [(source, source ^ distance) for source in range(lax.axis_size(axis))]
    return lax.ppermute(value, axis, pairs)


def others(part, axis):
    return [from_partner(part, axis, distance) for distance in range(1, lax.axis_size(axis))]


def forward_kernel(turn, width, pattern_ref, place_ref, *refs):
    slabs = refs[:LEVELS]
    latent_ref, weight_ref, left_ref, cot_ref = refs[LEVELS : LEVELS + 4]
    act_ref, grad_ref, sums_ref, back_ref = refs[-4:]
    step = pl.program_id(0)
    first = chunk_step(place_ref, turn, step) * STEP

    def picked(row):
        column = lax.rem(pattern_ref[first + row, 0], width)
        lanes = pl.ds(pl.multiple_of(column * BLK, BLK), BLK)
        return jnp.concatenate([slab[:, lanes] for slab in slabs], axis=1)

    across = (((1,), (1,)), ((), ()))
    along = (((0,), (0,)), ((), ()))
    every = [slice(row * BLK, (row + 1) * BLK) for row in range(STEP)]
    low = lax.dot_general(latent_ref[...], left_ref[...], across, preferred_element_type=F32)
    pres = []
    for row, rows in enumerate(every):
        sparse = lax.dot_general(picked(row), weight_ref[rows, :], across, preferred_element_type=F32)
        pres.append(sparse + low[:, rows])
    grads = []
    for pre, rows in zip(pres, every):
        square = pre * pre
        half = 0.5 + 0.5 * jnp.tanh(pre * (GELU_K + (GELU_K * GELU_A) * square))
        act = pre * half
        act_ref[:, rows] = act.astype(BF16)
        slope = half + act * (1.0 - half) * (2.0 * GELU_K + (6.0 * GELU_K * GELU_A) * square)
        grad = (cot_ref[:, rows].astype(F32) * slope).astype(BF16)
        grad_ref[:, rows] = grad
        grads.append(grad)
    sparse_cols = LEVELS * BLK
    for row, rows in enumerate(every):
        sums_ref[rows, :sparse_cols] = lax.dot_general(
            grads[row], picked(row), along, preferred_element_type=F32
        ).astype(BF16)
    grads = jnp.concatenate(grads, axis=1)
    sums_ref[:, sparse_cols:] = lax.dot_general(
        grads, latent_ref[...], along, preferred_element_type=F32
    ).astype(BF16)
    back = jnp.dot(grads, left_ref[...], preferred_element_type=F32)

    @pl.when(step == 0)
    def _():
        back_ref[...] = back

    @pl.when(step > 0)
    def _():
        back_ref[...] += back


def chunk_step(place, turn, step):
    per_chunk = place[0]
    return place[1 + turn + step // per_chunk] * per_chunk + lax.rem(step, per_chunk)


def chunk_group(place, turn):
    return place[1 + CHUNKS + turn]


def forward_chunk(turn, steps, width, pattern, place, slabs, moves, latent, weights, left, cot, carried, after=()):
    tok_rows, hidden = cot.shape
    rank = left.shape[1]
    wide = STEP * BLK
    rows = steps * wide
    at_slab = lambda move: (lambda i, p, w: (0, 0 if move is None else chunk_group(w, turn) ^ move))
    in_specs = [pl.BlockSpec((tok_rows, width * BLK), at_slab(move)) for move in moves] + [
        pl.BlockSpec((tok_rows, rank), lambda i, p, w: (0, 0)),
        pl.BlockSpec((wide, LEVELS * BLK), lambda i, p, w: (chunk_step(w, turn, i), 0)),
        pl.BlockSpec((wide, rank), lambda i, p, w: (chunk_step(w, turn, i), 0)),
        pl.BlockSpec((tok_rows, wide), lambda i, p, w: (0, chunk_step(w, turn, i))),
    ]
    operands = [pattern, place, *slabs, latent, weights, left, cot]
    aliases = {}
    if carried is not None:
        aliases = {len(operands): 0, len(operands) + 1: 1}
        operands += list(carried)
    operands += list(after)
    in_specs += [pl.BlockSpec(memory_space=pl.ANY)] * (len(operands) - 2 - len(in_specs))
    out_cols = LEVELS * BLK + rank
    return pl.pallas_call(
        functools.partial(forward_kernel, turn, width),
        grid_spec=pltpu.PrefetchScalarGridSpec(
            num_scalar_prefetch=2,
            grid=(steps,),
            in_specs=in_specs,
            out_specs=[
                pl.BlockSpec((tok_rows, wide), lambda i, p, w: (0, chunk_step(w, turn, i))),
                pl.BlockSpec((tok_rows, wide), lambda i, p, w: (0, chunk_step(w, turn, i))),
                pl.BlockSpec((wide, out_cols), lambda i, p, w: (i, 0)),
                pl.BlockSpec((tok_rows, rank), lambda i, p, w: (0, 0)),
            ],
        ),
        out_shape=[
            jax.ShapeDtypeStruct((tok_rows, hidden), BF16),
            jax.ShapeDtypeStruct((tok_rows, hidden), BF16),
            jax.ShapeDtypeStruct((rows, out_cols), BF16),
            jax.ShapeDtypeStruct((tok_rows, rank), F32),
        ],
        input_output_aliases=aliases,
        compiler_params=pltpu.CompilerParams(vmem_limit_bytes=VMEM),
        cost_estimate=pl.CostEstimate(flops=COST, bytes_accessed=24 << 20, transcendentals=0),
        name="forward_chunk",
    )(*operands)


def spread_kernel(turn, steps, width, moves, levels, last, pattern_ref, place_ref, grad_ref, weight_ref, *refs):
    out_ref, total = refs[-2], refs[-1]
    step = pl.program_id(0)
    first = chunk_step(place_ref, turn, step) * STEP
    span = width * BLK

    @pl.when(step == 0)
    def _():
        total[...] = jnp.zeros_like(total)

    weights = weight_ref[...]
    weights = jnp.concatenate([weights[:, level * BLK : (level + 1) * BLK] for level in levels], axis=1)
    every = [slice(row * BLK, (row + 1) * BLK) for row in range(STEP)]
    terms = [jnp.dot(grad_ref[:, cols], weights[cols, :], preferred_element_type=F32) for cols in every]
    for row in range(STEP):
        column = lax.rem(pattern_ref[first + row, 0], width)
        for at, level in enumerate(levels):
            begin = step_group(place_ref, turn, step) ^ moves[level] if last else at
            lanes = pl.ds(pl.multiple_of(begin * span + column * BLK, BLK), BLK)
            total[:, lanes] += terms[row][:, at * BLK : (at + 1) * BLK]

    @pl.when(step == steps - 1)
    def _():
        value = total[...]
        if last:
            value = value + lax.dot_general(
                refs[0][...], refs[1][...], (((1,), (1,)), ((), ())), preferred_element_type=F32
            )
        out_ref[...] = value.astype(BF16)


def step_group(place, turn, step):
    return place[1 + CHUNKS + turn + step // place[0]]


def spread(turn, steps, width, pattern, place, grad, weights, moves, levels, extra, out_cols, after=()):
    tok_rows = grad.shape[0]
    wide = STEP * BLK
    return pl.pallas_call(
        functools.partial(spread_kernel, turn, steps, width, tuple(moves), tuple(levels), bool(extra)),
        grid_spec=pltpu.PrefetchScalarGridSpec(
            num_scalar_prefetch=2,
            grid=(steps,),
            in_specs=[
                pl.BlockSpec((tok_rows, wide), lambda i, p, w: (0, chunk_step(w, turn, i))),
                pl.BlockSpec((wide, LEVELS * BLK), lambda i, p, w: (chunk_step(w, turn, i), 0)),
            ]
            + [pl.BlockSpec(value.shape, lambda i, p, w: (0, 0)) for value in extra]
            + [pl.BlockSpec(memory_space=pl.ANY)] * len(after),
            out_specs=pl.BlockSpec((tok_rows, out_cols), lambda i, p, w: (0, 0)),
            scratch_shapes=[pltpu.VMEM((tok_rows, out_cols), F32)],
        ),
        out_shape=jax.ShapeDtypeStruct((tok_rows, out_cols), BF16),
        compiler_params=pltpu.CompilerParams(vmem_limit_bytes=VMEM),
        cost_estimate=pl.CostEstimate(flops=COST, bytes_accessed=24 << 20, transcendentals=0),
        name="spread",
    )(pattern, place, grad, weights, *extra, *after)


def merge_kernel(remote, distances, span, place_ref, own_ref, *refs):
    sources, out_ref = refs[:-1], refs[-1]
    owner = pl.program_id(0)
    for turn in range(len(sources)):
        lanes = pl.ds(pl.multiple_of((chunk_group(place_ref, 0) ^ turn) * span, span), span)
        total = own_ref[owner, :, lanes].astype(F32)
        for at, level in enumerate(remote):
            total = total + sources[turn][owner ^ distances[level], :, at * span : (at + 1) * span].astype(F32)
        out_ref[0, :, lanes] = total.astype(BF16)


def merge_terms(place, own, arrived, remote, distances, span):
    count, rows, width = own.shape
    return pl.pallas_call(
        functools.partial(merge_kernel, tuple(remote), tuple(distances), span),
        grid_spec=pltpu.PrefetchScalarGridSpec(
            num_scalar_prefetch=1,
            grid=(count,),
            in_specs=[pl.BlockSpec(value.shape, lambda q, w: (0, 0, 0)) for value in (own, *arrived)],
            out_specs=pl.BlockSpec((1, rows, width), lambda q, w: (0, 0, q)),
        ),
        out_shape=jax.ShapeDtypeStruct((1, rows, count * width), BF16),
        compiler_params=pltpu.CompilerParams(vmem_limit_bytes=VMEM),
        name="merge_terms",
    )(place, own, *arrived)


def right_kernel(place_ref, tokens_ref, back_ref, *outs):
    cols = outs[0].shape[1]
    for turn in range(CHUNKS):
        lanes = pl.ds(pl.multiple_of(place_ref[1 + turn] * cols, cols), cols)
        outs[turn % 2][turn // 2] = lax.dot_general(
            tokens_ref[:, lanes], back_ref[...], (((0,), (0,)), ((), ())), preferred_element_type=F32
        ).astype(BF16)


def right_sums(place, tokens, back):
    shape = jax.ShapeDtypeStruct((CHUNKS // 2, tokens.shape[1] // CHUNKS, back.shape[1]), BF16)
    return pl.pallas_call(
        right_kernel,
        grid_spec=pltpu.PrefetchScalarGridSpec(
            num_scalar_prefetch=1,
            grid=(1,),
            in_specs=[pl.BlockSpec(value.shape, lambda i, w: (0, 0)) for value in (tokens, back)],
            out_specs=[pl.BlockSpec(shape.shape, lambda i, w: (0, 0, 0))] * 2,
        ),
        out_shape=[shape, shape],
        compiler_params=pltpu.CompilerParams(vmem_limit_bytes=VMEM),
        name="right_sums",
    )(place, tokens, back)


def pair_kernel(place_ref, *refs):
    for mine, other, out in zip(refs[:2], refs[2:4], refs[4:]):
        out[...] = (mine[...].astype(F32) + other[...].astype(F32)).astype(out.dtype)


def pair_sums(place, total, swapped, index, bits, dtypes):
    count = 1 << bits
    rows = total.shape[0] // 2 // count
    cols = total.shape[1]
    block = (rows // 2, cols)
    specs = [
        pl.BlockSpec(block, lambda i, h, w, turn=turn: ((turn * count + 2 * i + w[1 + 2 * CHUNKS]) * 2 + h, 0))
        for turn in (0, 1)
    ]
    sums = pl.pallas_call(
        pair_kernel,
        grid_spec=pltpu.PrefetchScalarGridSpec(
            num_scalar_prefetch=1,
            grid=(count // 2, 2),
            in_specs=specs * 2,
            out_specs=[pl.BlockSpec(block, lambda i, h, w: (2 * i + h, 0))] * 2,
        ),
        out_shape=[jax.ShapeDtypeStruct((rows * count // 2, cols), dtype) for dtype in dtypes],
        name="pair_sums",
    )(place, total, total, swapped, swapped)
    if bits == 1:
        return sums
    return [lower_sums(part.astype(F32).reshape(count // 2, rows, cols), index, 1, bits).astype(part.dtype) for part in sums]


def final_kernel(scale, kept_ref, first_ref, second_ref, blocks_ref, left_ref):
    total = kept_ref[...] + first_ref[...].astype(F32) + second_ref[...].astype(F32)
    total = total * scale
    cols = blocks_ref.shape[1]
    blocks_ref[...] = total[:, :cols]
    left_ref[...] = total[:, cols:]


def final_sums(kept, first, second, scale):
    rows, cols = kept.shape
    split = LEVELS * BLK
    block = lambda width: pl.BlockSpec((rows // 2, width), lambda h: (h, 0))
    return pl.pallas_call(
        functools.partial(final_kernel, scale),
        grid=(2,),
        in_specs=[block(cols)] * 3,
        out_specs=[block(split), block(cols - split)],
        out_shape=[jax.ShapeDtypeStruct((rows, width), F32) for width in (split, cols - split)],
        name="final_sums",
    )(kept, first, second)


def lower_sums(part, index, first, bits):
    for bit in range(first, bits):
        mine = (index >> bit) & 1
        part = part.reshape(part.shape[0] // 2, 2, *part.shape[1:])
        keep = lax.dynamic_index_in_dim(part, mine, 1, keepdims=False)
        send = lax.dynamic_index_in_dim(part, 1 - mine, 1, keepdims=False)
        part = keep + from_partner(send.astype(BF16), "seq", 1 << bit).astype(F32)
    return part[0]


def local(tokens, block_weights, left_factor, right_factor, pattern, cotangent):
    tok_rows, local_width = tokens.shape
    feat_count = lax.axis_size("feat")
    seq_count = lax.axis_size("seq")
    norm_scale = 1.0 / math.sqrt(tok_rows * seq_count)
    local_blocks = local_width // BLK
    width = local_blocks * feat_count // GROUPS
    groups = local_blocks // width
    rows = pattern.shape[0] // groups
    span = width * BLK
    strides = [0] + [GROUPS >> level for level in range(1, LEVELS)]
    distances = [stride // groups for stride in strides]
    moves = [stride if stride < groups else 0 for stride in strides]

    index = lax.axis_index("seq")
    bits = seq_count.bit_length() - 3
    near, far = 1 << bits, 2 << bits
    quarter = index >> bits

    latent_part = jnp.dot(tokens, right_factor, preferred_element_type=F32)
    distance = feat_count // 2
    other = from_partner(latent_part.astype(BF16), "feat", distance)
    received = []
    for turn in range(groups):
        group = (quarter ^ (CHUNKS - 1)) * groups // CHUNKS ^ turn
        piece = lax.dynamic_slice_in_dim(tokens, group * span, span, 1)
        if turn == 0:
            late, other = lax.optimization_barrier((piece, other))
        else:
            piece, latent_part = lax.optimization_barrier((piece, latent_part))
            late = piece
        sources = [late if d == feat_count // 2 else piece for d in distances]
        received.append([from_partner(s, "feat", d) if d > 0 else None for s, d in zip(sources, distances)])
        if turn == 0:
            latent_part = latent_part + other.astype(F32)
            while distance > 1:
                distance //= 2
                latent_part = latent_part + from_partner(latent_part.astype(BF16), "feat", distance).astype(F32)
    latent = latent_part.astype(BF16)

    remote = [level for level in range(LEVELS) if distances[level] > 0]
    slots = [None if d > 0 else move for d, move in zip(distances, moves)]
    steps = pattern.shape[0] // STEP // CHUNKS
    turns = CHUNKS // groups
    part_rows = tok_rows // feat_count

    def to_owner(value):
        value = value.reshape(feat_count, part_rows, value.shape[1])
        return lax.all_to_all(value, "feat", split_axis=0, concat_axis=0, tiled=True)

    chunks = [quarter ^ (CHUNKS - 1 - turn) for turn in range(CHUNKS)]
    place = jnp.stack([jnp.int32(steps)] + chunks + [chunk * groups // CHUNKS for chunk in chunks] + [index & 1]).astype(jnp.int32)

    def forward(turn, count, carried, after=()):
        slabs = [tokens if slab is None else slab for slab in received[turn // turns]]
        return forward_chunk(
            turn, steps * count, width, pattern, place, slabs, slots, latent, block_weights, left_factor, cotangent,
            carried, after,
        )

    def spread_levels(turn, count, grad, levels, extra, out_cols, after=()):
        return spread(
            turn, steps * count, width, pattern, place, grad, block_weights, moves, levels, extra, out_cols, after
        )

    hold = lax.optimization_barrier
    near_hop = lambda value: from_partner(value, "seq", near)
    far_hop = lambda value: from_partner(value, "seq", far)

    def line_hop(value, routes):
        low = range(near)
        pairs = [(a * near + at, b * near + at) for a, b in routes for at in low]
        return lax.ppermute(value, "seq", pairs)

    inward = lambda value: line_hop(value, [(0, 1), (3, 2)])
    across = lambda value: line_hop(value, [(1, 2), (2, 1)])
    core_hop = lambda value: from_partner(value, "seq", 1)
    wide = lambda value: value.astype(F32)

    act, grad, total, back = forward(0, 2, None)
    if groups > 1:
        received[1], total, grad = hold((received[1], total, grad))
    swapped = core_hop(total)
    arrived = []
    if groups > 1:
        terms = spread_levels(0, turns, grad, remote, (), len(remote) * span)
        terms, swapped, grad = hold((terms, swapped, grad))
    sum0, sum1 = pair_sums(place, total, swapped, index, bits, (BF16, BF16))
    got0, got1 = inward(sum0), inward(sum1)
    if groups > 1:
        arrived.append(to_owner(terms))
    act, grad, total, more = forward(2, 2, (act, grad))
    grad, total, more, got0, arrived = hold((grad, total, more, got0, arrived))

    got2 = across((wide(sum1) + wide(got0)).astype(BF16))
    back = back + more
    parts = others(back.astype(BF16), "feat")
    swapped = core_hop(total)
    terms = spread_levels(CHUNKS - turns, turns, grad, remote, (), len(remote) * span)
    terms, swapped, parts, grad = hold((terms, swapped, parts, grad))

    for part in parts:
        back = back + wide(part)
    back_latent = back.astype(BF16)
    right_send, right_keep = right_sums(place, tokens, back_latent)
    close = near_hop(right_send)
    arrived.append(to_owner(terms))
    sum2, sum3 = pair_sums(place, total, swapped, index, bits, (BF16, F32))
    own_levels = [level for level in range(LEVELS) if level not in remote]
    own = spread_levels(0, CHUNKS, grad, own_levels, (back_latent, right_factor), local_width, (sum3,))
    own, close, got1, got2 = hold((own, close, got1, got2))

    last_part = far_hop((wide(right_keep[0]) + wide(close[0])).astype(BF16))
    send4 = (wide(sum2) + wide(got2)).astype(BF16)
    send3 = (wide(sum0) + wide(got1)).astype(BF16)
    own, send4, send3 = hold((own, send4, send3))
    own = to_owner(own)
    send4, send3, last_part = hold((send4, send3, last_part))
    got4 = near_hop(send4)
    got3 = across(send3)
    right = wide(right_keep[1]) + wide(close[1]) + wide(last_part)
    grad_right = lower_sums(right.reshape(1 << bits, -1, right.shape[1]), index, 0, bits) * norm_scale
    grad_input = merge_terms(place, own, arrived, remote, distances, span)
    grad_input, grad_right, got3, got4 = hold((grad_input, grad_right, got3, got4))
    grad_blocks, grad_left = final_sums(sum3, got3, got4, norm_scale)

    return (act, grad_input, grad_blocks, grad_left, grad_right)


def solution(mesh):
    in_specs = (
        P("seq", "feat"),
        P("feat", None),
        P("feat", None),
        P("feat", None),
        P("feat", None),
        P("seq", "feat"),
    )
    out_specs = (
        P("seq", "feat"),
        P("seq", "feat", None),
        P(("feat", "seq"), None),
        P(("feat", "seq"), None),
        P(("feat", "seq"), None),
    )
    return jax.shard_map(local, mesh=mesh, in_specs=in_specs, out_specs=out_specs, check_vma=False)
```
